32 devices in a mesh: grp: 4 (over x, core), sub: 8 (over z, y).
Axes of the slice: x: 2, y: 2, z: 4, core: 2. Of those that a mesh axis runs over, the one named last changes fastest.
Arguments:
- loads: float32 [32, 8, 1024], P(('grp', 'sub')), may hold values from -6 to 6
- schur: bfloat16 [32, 1024, 1024], P(('grp', 'sub')), may hold values from -0.1875 to 0.1875
- neumann: bfloat16 [32, 1024, 1024], P(('grp', 'sub')), may hold values from -0.1875 to 0.1875
- basis: float32 [32, 24, 1024], P(('grp', 'sub')), may hold values from -0.375 to 0.375
- coarse_index: int32 [32, 24], P(('grp', 'sub')), may hold values from 0 to 127
- coarse_inverse: float32 [128, 128], P(('grp', 'sub')), may hold values from -1 to 3
Outputs:
- solution: float32 [32, 8, 1024], P(('grp', 'sub'))
- residual: float32 [32, 8, 1024], P(('grp', 'sub'))
The draws below stay inside these ranges and needn't reach their ends.
All inputs are finite; a program needn't handle non-finite values.
Results may differ from the reference program's by a relative error of at most 0.00063.
Values sent between devices are 32-bit elements; how exact they have to be, the bound alone decides.
A program may use at most 64 MiB of HBM per device.

```python
import jax
import jax.numpy as jnp
from jax import lax

IFACE = 1024
RIM = 256
NCRN = 24
LOADS = 8
ITERS = 1
SUBS = 32
COARSE = 128
N_GRP = 4
N_SUB = 8


def draw_coarse_inverse(key, part):
    first_key, second_key = jax.random.split(jax.random.fold_in(key, 17))
    diagonal = jax.random.uniform(first_key, (COARSE,), jnp.float32, 0.5, 2.0)
    mixing = jax.random.normal(second_key, (COARSE, COARSE), jnp.float32) * (0.6 / COARSE ** 0.5)
    return jnp.diag(diagonal) + mixing


def with_ends(drawn, rng, low, top_value):
    place = [jax.random.randint(jax.random.fold_in(rng, axis), (), 0, length) for axis, length in enumerate(drawn.shape)]
    widest = drawn.shape.index(max(drawn.shape))
    beside = place[:widest] + [(place[widest] + 1) % drawn.shape[widest]] + place[widest + 1:]
    return drawn.at[tuple(place)].set(low).at[tuple(beside)].set(top_value)


def block_scale(key, extent, pieces, low, top_value):
    factor_of = 1.0
    for axis_at, parts in pieces:
        steps = jax.random.uniform(jax.random.fold_in(jax.random.fold_in(key, 6), axis_at), (parts,), jnp.float32, low / len(pieces), top_value / len(pieces))
        factor_of = factor_of * jnp.repeat(jnp.exp(steps), extent[axis_at] // parts).reshape((-1,) + (1,) * (len(extent) - 1 - axis_at))
    return factor_of


def bell_draw(key, shape, scale, bound, cuts=(), kind=jnp.bfloat16):
    loudness = block_scale(key, shape, cuts, -0.22, 0.18) if cuts else 1.0
    entries = jax.random.normal(key, shape, jnp.float32) * scale * loudness
    return jnp.minimum(jnp.maximum(entries, -bound), bound).astype(kind)


def setup_inputs(seed: int = 0) -> dict:
    arg_keys = jax.random.split(jax.random.key(seed), 7)
    loads = bell_draw(arg_keys[0], (SUBS, LOADS, IFACE), 1.0, 6.0, ((0, 32),), jnp.float32)
    schur = bell_draw(arg_keys[1], (SUBS, IFACE, IFACE), IFACE ** -0.5, 0.1875, ((0, 32),))
    neumann = bell_draw(arg_keys[2], (SUBS, IFACE, IFACE), IFACE ** -0.5, 0.1875, ((0, 32),))
    basis = bell_draw(arg_keys[3], (SUBS, NCRN, IFACE), (IFACE // 4) ** -0.5, 0.375, ((0, 32),), jnp.float32)
    coarse_index = with_ends(jax.random.randint(arg_keys[4], (SUBS, NCRN), 0, COARSE), jax.random.fold_in(arg_keys[4], 1), 0, COARSE - 1).astype(jnp.int32)
    coarse_inverse = draw_coarse_inverse(jax.random.fold_in(arg_keys[6], 71), 0)
    return dict(loads=loads, schur=schur, neumann=neumann, basis=basis, coarse_index=coarse_index, coarse_inverse=coarse_inverse)


def assemble(field):
    chains = field.reshape(N_GRP, N_SUB, LOADS, IFACE)
    zeros = jnp.zeros((N_GRP, 1, LOADS, RIM), field.dtype)
    from_left = jnp.concatenate([zeros, chains[:, :-1, :, IFACE - RIM:]], axis=1)
    from_right = jnp.concatenate([chains[:, 1:, :, :RIM], zeros], axis=1)
    middle = chains[:, :, :, RIM:IFACE - RIM]
    joined = jnp.concatenate([chains[:, :, :, :RIM] + from_left, middle, chains[:, :, :, IFACE - RIM:] + from_right], axis=3)
    return joined.reshape(field.shape)


def rim_weights(dtype):
    position = jnp.arange(N_GRP * N_SUB, dtype=jnp.int32) % N_SUB
    columns = jnp.arange(IFACE, dtype=jnp.int32)
    lower_rim = (columns[None, :] < RIM) & (position[:, None] > 0)
    upper_rim = (columns[None, :] >= IFACE - RIM) & (position[:, None] < N_SUB - 1)
    weights = jnp.where(lower_rim | upper_rim, 0.5, 1.0).astype(dtype)
    return weights[:, None, :]


def local_products(field, matrices, diagonal_scale, factor):
    def single(operands):
        vector, matrix = operands
        product = jnp.dot(vector.astype(jnp.bfloat16), matrix, preferred_element_type=jnp.float32)
        return diagonal_scale * vector + factor * product.astype(vector.dtype)
    return lax.map(single, (field, matrices))


def reference(loads, schur, neumann, basis, coarse_index, coarse_inverse):
    weights = rim_weights(loads.dtype)
    force = assemble(loads)
    high = lax.Precision.HIGHEST

    def precondition(resid):
        weighted = weights * resid
        neumann_part = local_products(weighted, neumann, 0.25, 0.0625)
        coarse_terms = jnp.einsum('sli,ski->skl', weighted, basis, precision=high)
        flat_terms = coarse_terms.reshape(SUBS * NCRN, LOADS)
        coarse_residual = jax.ops.segment_sum(flat_terms, coarse_index.reshape(-1).astype(jnp.int32), num_segments=COARSE)
        coarse_value = jnp.dot(coarse_residual.T, coarse_inverse, precision=high)
        picked = coarse_value.T[coarse_index.astype(jnp.int32)]
        coarse_part = jnp.einsum('skl,ski->sli', picked, basis, precision=high)
        return assemble(weights * (neumann_part + coarse_part))

    solution = jnp.zeros_like(loads)
    residual = force
    for sweep in range(ITERS):
        solution = solution + precondition(residual)
        residual = force - assemble(local_products(solution, schur, 4.0, 1.0))
    return solution, residual
```

```python
import functools

import jax
import jax.numpy as jnp
from jax import lax
from jax.experimental import pallas as pl
from jax.experimental.pallas import tpu as pltpu
from jax.sharding import PartitionSpec as P

RIM = 256
MESH = pl.DeviceIdType.MESH
GATHERED_LIMIT = 1 << 20
BF16 = jnp.bfloat16
F32 = jnp.float32
NN = (((1,), (0,)), ((), ()))
NT = (((1,), (1,)), ((), ()))


def split(x):
    high = x.astype(BF16)
    return high, (x - high.astype(F32)).astype(BF16)


def dot(a, b, dims=NN):
    return lax.dot_general(a, b, dims, preferred_element_type=F32)


def thin_dot(a, b_high, b_low, dims=NN):
    rows = a.shape[0]
    high, low = split(a)
    both = dot(jnp.concatenate([high, low], axis=0), b_high, dims)
    return both[:rows] + both[rows:] + dot(high, b_low, dims)


def kernel(
    n_grp, n_sub,
    loads_hbm, schur_hbm, neumann_hbm, basis_hbm, index_hbm, inverse_hbm,
    solution_hbm, residual_hbm,
    loads, schur, neumann, basis, index, inverse_parts, inverse,
    loads_in, basis_in, index_in, part_in, result_in,
    e_high, e_low, h_high, h_low, part, result, solution, residual,
    terms, terms_grp, group_terms, terms_sub,
    local_sem, halo_send, halo_recv, grp_send, grp_recv, sub_send, sub_recv,
    inv_sub_send, inv_sub_recv, inv_grp_send, inv_grp_recv,
):
    width = loads.shape[1]
    coarse = inverse.shape[0]
    rows = inverse_parts.shape[2]
    g = lax.axis_index("grp")
    b = lax.axis_index("sub")
    grp_peers = [lax.rem(g + k, n_grp) for k in range(1, n_grp)]
    sub_peers = [lax.rem(b + k, n_sub) for k in range(1, n_sub)]
    has_left = b > 0
    has_right = b < n_sub - 1
    first = pl.ds(0, RIM)
    last = pl.ds(width - RIM, RIM)

    barrier = pltpu.get_barrier_semaphore()
    for peer in sub_peers:
        pl.semaphore_signal(barrier, inc=1, device_id=(g, peer), device_id_type=MESH)
    for peer in grp_peers:
        pl.semaphore_signal(barrier, inc=1, device_id=(peer, b), device_id_type=MESH)

    def fetch(source, target, at):
        copy = pltpu.make_async_copy(source, target, local_sem.at[at])
        copy.start()
        return copy

    loads_copy = fetch(loads_hbm.at[0], loads, 0)
    basis_copy = fetch(basis_hbm.at[0], basis, 1)
    index_copy = fetch(index_hbm, index, 2)
    inverse_copy = fetch(inverse_hbm, inverse_parts.at[g, b], 3)
    neumann_copy = fetch(neumann_hbm.at[0], neumann, 4)
    schur_copy = fetch(schur_hbm.at[0], schur, 5)

    def remote(source, target, send, recv, device):
        return pltpu.make_async_remote_copy(
            src_ref=source, dst_ref=target, send_sem=send, recv_sem=recv,
            device_id=device, device_id_type=MESH,
        )

    left_id = (g, lax.max(b - 1, 0))
    right_id = (g, lax.min(b + 1, n_sub - 1))

    def halo(lower, upper, landing, at):
        to_right = remote(upper, landing.at[0], halo_send.at[at, 0], halo_recv.at[at, 0], right_id)
        to_left = remote(lower, landing.at[1], halo_send.at[at, 1], halo_recv.at[at, 1], left_id)

        def start():
            pl.when(has_right)(lambda: to_right.start())
            pl.when(has_left)(lambda: to_left.start())

        def wait_recv():
            pl.when(has_left)(lambda: to_right.wait_recv())
            pl.when(has_right)(lambda: to_left.wait_recv())

        def wait_send():
            pl.when(has_right)(lambda: to_right.wait_send())
            pl.when(has_left)(lambda: to_left.wait_send())

        return start, wait_recv, wait_send

    def clear(slot):
        loads_in[slot] = jnp.zeros(loads_in.shape[1:], F32)
        basis_in[slot] = jnp.zeros(basis_in.shape[1:], F32)
        index_in[slot] = jnp.zeros(index_in.shape[1:], jnp.int32)
        part_in[slot] = jnp.zeros(part_in.shape[1:], F32)
        result_in[slot] = jnp.zeros(result_in.shape[1:], F32)

    pl.when(jnp.logical_not(has_left))(lambda: clear(0))
    pl.when(jnp.logical_not(has_right))(lambda: clear(1))

    loads_halo = halo(loads.at[:, first], loads.at[:, last], loads_in, 0)
    basis_halo = halo(basis.at[:, first], basis.at[:, last], basis_in, 1)
    index_halo = halo(index, index, index_in, 2)
    part_halo = halo(part.at[:, first], part.at[:, last], part_in, 3)
    result_halo = halo(result.at[:, first], result.at[:, last], result_in, 4)

    loads_copy.wait()
    pl.semaphore_wait(barrier, n_grp + n_sub - 2)
    loads_halo[0]()
    index_copy.wait()
    index_halo[0]()
    basis_copy.wait()
    basis_halo[0]()
    inverse_copy.wait()
    inv_sub = [
        remote(inverse_parts.at[g, b], inverse_parts.at[g, b], inv_sub_send.at[k], inv_sub_recv.at[k], (g, peer))
        for k, peer in enumerate(sub_peers)
    ]
    for copy in inv_sub:
        copy.start()

    def expand(index_row, functions):
        place = lax.broadcasted_iota(jnp.int32, (coarse, index_row.shape[1]), 0)
        chosen = jnp.where(place == index_row, 1.0, 0.0).astype(BF16)
        high, low = split(functions)
        return dot(chosen, high) + dot(chosen, low)

    columns = lax.broadcasted_iota(jnp.int32, (1, width), 1)
    shared = ((columns < RIM) & has_left) | ((columns >= width - RIM) & has_right)
    weights = jnp.where(shared, 0.5, 1.0).astype(F32)

    expanded = expand(index[...], basis[...])
    high, low = split(expanded)
    e_high[...] = high
    e_low[...] = low

    loads_halo[1]()

    def assembled(field, landed):
        return jnp.concatenate(
            [field[:, :RIM] + landed[0], field[:, RIM : width - RIM], field[:, width - RIM :] + landed[1]], axis=1
        )

    force = assembled(loads[...], loads_in)
    weighted = weights * force
    terms[...] = thin_dot(weighted, e_high[...], e_low[...], NT)
    to_grp = [
        remote(terms, terms_grp.at[k], grp_send.at[k], grp_recv.at[k], (peer, b))
        for k, peer in enumerate(grp_peers)
    ]
    for copy in to_grp:
        copy.start()

    neumann_copy.wait()
    rounded = weighted.astype(BF16)

    def neumann_columns(at, size):
        product = dot(rounded, neumann[:, at : at + size])
        here = weighted[:, at : at + size]
        part[:, at : at + size] = weights[:, at : at + size] * (0.25 * here + 0.0625 * product)

    neumann_columns(0, RIM)
    neumann_columns(width - RIM, RIM)
    part_halo[0]()

    total = terms[...]
    for k, copy in enumerate(to_grp):
        copy.wait_recv()
        total = total + terms_grp[k]
    group_terms[...] = total
    to_sub = [
        remote(group_terms, terms_sub.at[k], sub_send.at[k], sub_recv.at[k], (g, peer))
        for k, peer in enumerate(sub_peers)
    ]
    for copy in to_sub:
        copy.start()

    for copy in inv_sub:
        copy.wait_recv()
    inv_grp = [
        remote(inverse_parts.at[g], inverse_parts.at[g], inv_grp_send.at[k], inv_grp_recv.at[k], (peer, b))
        for k, peer in enumerate(grp_peers)
    ]
    for copy in inv_grp:
        copy.start()

    neumann_columns(RIM, width - 2 * RIM)

    basis_halo[1]()
    index_halo[1]()
    own = weights * (e_high[...].astype(F32) + e_low[...].astype(F32))
    from_left = own[:, :RIM] + 0.5 * expand(index_in[0], basis_in[0])
    from_right = own[:, width - RIM :] + 0.5 * expand(index_in[1], basis_in[1])
    f_high, f_low = split(jnp.concatenate([from_left, own[:, RIM : width - RIM], from_right], axis=1))
    for copy in inv_grp:
        copy.wait_recv()
    for i in range(n_grp):
        for j in range(n_sub):
            at = (i * n_sub + j) * rows
            inverse[at : at + rows, :] = inverse_parts[i, j]
    i_high, i_low = split(inverse[...])
    h = dot(i_high, f_high) + dot(i_high, f_low) + dot(i_low, f_high)
    high, low = split(h)
    h_high[...] = high
    h_low[...] = low

    part_halo[1]()
    base = assembled(part[...], part_in)

    total = group_terms[...]
    for k, copy in enumerate(to_sub):
        copy.wait_recv()
        total = total + terms_sub[k]
    found = base + thin_dot(total, h_high[...], h_low[...])
    solution[...] = found
    solution_copy = pltpu.make_async_copy(solution, solution_hbm.at[0], local_sem.at[6])
    solution_copy.start()

    schur_copy.wait()
    rounded_solution = found.astype(BF16)

    def schur_columns(at, size):
        product = dot(rounded_solution, schur[:, at : at + size])
        return 4.0 * found[:, at : at + size] + product

    low_rim = schur_columns(0, RIM)
    high_rim = schur_columns(width - RIM, RIM)
    result[:, :RIM] = low_rim
    result[:, width - RIM :] = high_rim
    result_halo[0]()
    residual[:, RIM : width - RIM] = force[:, RIM : width - RIM] - schur_columns(RIM, width - 2 * RIM)
    for copy in inv_sub + inv_grp + to_grp + to_sub:
        copy.wait_send()
    for each in (loads_halo, basis_halo, index_halo, part_halo):
        each[2]()
    result_halo[1]()
    residual[:, :RIM] = force[:, :RIM] - (low_rim + result_in[0])
    residual[:, width - RIM :] = force[:, width - RIM :] - (high_rim + result_in[1])
    residual_copy = pltpu.make_async_copy(residual, residual_hbm.at[0], local_sem.at[7])
    residual_copy.start()
    result_halo[2]()
    solution_copy.wait()
    residual_copy.wait()


def fused(loads, schur, neumann, basis, coarse_index, coarse_inverse):
    n_grp, n_sub = lax.axis_size("grp"), lax.axis_size("sub")
    _, cases, width = loads.shape
    corners = basis.shape[1]
    rows, coarse = coarse_inverse.shape
    dma = pltpu.SemaphoreType.DMA
    field = pltpu.VMEM((cases, width), F32)
    rims = pltpu.VMEM((2, cases, RIM), F32)
    scratch = [
        field,
        pltpu.VMEM((width, width), BF16),
        pltpu.VMEM((width, width), BF16),
        pltpu.VMEM((corners, width), F32),
        pltpu.VMEM((1, corners), jnp.int32),
        pltpu.VMEM((n_grp, n_sub, rows, coarse), F32),
        pltpu.VMEM((coarse, coarse), F32),
        rims,
        pltpu.VMEM((2, corners, RIM), F32),
        pltpu.VMEM((2, 1, corners), jnp.int32),
        rims,
        rims,
        pltpu.VMEM((coarse, width), BF16),
        pltpu.VMEM((coarse, width), BF16),
        pltpu.VMEM((coarse, width), BF16),
        pltpu.VMEM((coarse, width), BF16),
        field,
        field,
        field,
        field,
        pltpu.VMEM((cases, coarse), F32),
        pltpu.VMEM((n_grp - 1, cases, coarse), F32),
        pltpu.VMEM((cases, coarse), F32),
        pltpu.VMEM((n_sub - 1, cases, coarse), F32),
        dma((8,)),
        dma((5, 2)),
        dma((5, 2)),
        dma((n_grp - 1,)),
        dma((n_grp - 1,)),
        dma((n_sub - 1,)),
        dma((n_sub - 1,)),
        dma((n_sub - 1,)),
        dma((n_sub - 1,)),
        dma((n_grp - 1,)),
        dma((n_grp - 1,)),
    ]
    out = jax.ShapeDtypeStruct(loads.shape, F32)
    return pl.pallas_call(
        functools.partial(kernel, n_grp, n_sub),
        out_shape=(out, out),
        in_specs=[pl.BlockSpec(memory_space=pl.ANY)] * 6,
        out_specs=(pl.BlockSpec(memory_space=pl.ANY),) * 2,
        scratch_shapes=scratch,
        compiler_params=pltpu.CompilerParams(
            collective_id=0, has_side_effects=True, vmem_limit_bytes=48 << 20
        ),
    )(loads, schur, neumann, basis, coarse_index, coarse_inverse)


def with_halo(x, sides, width):
    for axis, dim in sides:
        peers, length = (lax.axis_size(axis), x.shape[dim])
        up = [(i, (i + 1) % peers) for i in range(peers - 1)]
        down = [(j, i) for i, j in up]
        last = lax.slice_in_dim(x, length - width, length, axis=dim)
        first = lax.slice_in_dim(x, 0, width, axis=dim)
        before = lax.ppermute(last, axis, up)
        after = lax.ppermute(first, axis, down)
        x = jnp.concatenate([before, x, after], axis=dim)
    return x


def staged(loads, schur, neumann, basis, coarse_index, coarse_inverse):
    width = loads.shape[2]
    coarse_total = coarse_inverse.shape[1]
    high = lax.Precision.HIGHEST
    position = lax.axis_index("sub")
    final_index = lax.axis_size("sub") - 1
    columns = lax.broadcasted_iota(jnp.int32, (1, 1, width), 2)
    lower_rim = (columns < RIM) & (position > 0)
    upper_rim = (columns >= width - RIM) & (position < final_index)
    weights = jnp.where(lower_rim | upper_rim, 0.5, 1.0).astype(jnp.float32)
    selector = (
        coarse_index[0][:, None] == lax.broadcasted_iota(jnp.int32, (1, coarse_total), 1)
    ).astype(jnp.float32)

    def assemble(field):
        padded = with_halo(field, (("sub", 2),), RIM)
        from_left = padded[:, :, :RIM]
        from_right = padded[:, :, RIM + width :]
        middle = field[:, :, RIM : width - RIM]
        return jnp.concatenate(
            [field[:, :, :RIM] + from_left, middle, field[:, :, width - RIM :] + from_right], axis=2
        )

    force = assemble(loads)
    residual = force
    weighted = (weights * residual)[0]
    product = jnp.dot(weighted.astype(jnp.bfloat16), neumann[0], preferred_element_type=jnp.float32)
    neumann_part = 0.25 * weighted + 0.0625 * product
    coarse_terms = jnp.dot(weighted, basis[0].T, precision=high)
    partial_sums = jnp.dot(coarse_terms, selector, precision=high)
    owned = lax.psum_scatter(partial_sums, ("grp", "sub"), scatter_dimension=1, tiled=True)
    value_terms = jnp.dot(owned, coarse_inverse, precision=high)
    within = lax.psum(value_terms, "sub")
    coarse_value = lax.psum(within, "grp")
    picked = jnp.dot(coarse_value, selector.T, precision=high)
    combined = neumann_part + jnp.dot(picked, basis[0], precision=high)
    solution = assemble(weights * combined[None])
    product = jnp.dot(
        solution[0].astype(jnp.bfloat16), schur[0], preferred_element_type=jnp.float32
    )
    residual = force - assemble((4.0 * solution[0] + product)[None])
    return (solution, residual)


def local(loads, schur, neumann, basis, coarse_index, coarse_inverse):
    coarse_total = coarse_inverse.shape[1]
    form = fused if 4 * coarse_total * coarse_total <= GATHERED_LIMIT else staged
    return form(loads, schur, neumann, basis, coarse_index, coarse_inverse)


def solution(mesh):
    in_specs = (
        P(("grp", "sub"), None, None),
        P(("grp", "sub"), None, None),
        P(("grp", "sub"), None, None),
        P(("grp", "sub"), None, None),
        P(("grp", "sub"), None),
        P(("grp", "sub"), None),
    )
    out_specs = (P(("grp", "sub"), None, None), P(("grp", "sub"), None, None))
    return jax.shard_map(local, mesh=mesh, in_specs=in_specs, out_specs=out_specs, check_vma=False)
```

```python
import functools

import jax
import jax.numpy as jnp
from jax import lax
from jax.experimental import pallas as pl
from jax.experimental.pallas import tpu as pltpu
from jax.sharding import PartitionSpec as P

RIM = 256
MESH = pl.DeviceIdType.MESH
GATHERED_LIMIT = 1 << 20
BF16 = jnp.bfloat16
F32 = jnp.float32
NN = (((1,), (0,)), ((), ()))
NT = (((1,), (1,)), ((), ()))


def split(x):
    high = x.astype(BF16)
    return high, (x - high.astype(F32)).astype(BF16)


def dot(a, b, dims=NN):
    return lax.dot_general(a, b, dims, preferred_element_type=F32)


def thin_dot(a, b_high, b_low, dims=NN):
    rows = a.shape[0]
    high, low = split(a)
    both = dot(jnp.concatenate([high, low], axis=0), b_high, dims)
    return both[:rows] + both[rows:] + dot(high, b_low, dims)


def kernel(
    n_grp, n_sub,
    loads_hbm, schur_hbm, neumann_hbm, basis_hbm, index_hbm, inverse_hbm,
    solution, residual,
    loads, schur, neumann, basis, index, inverse_parts, inverse,
    loads_in, basis_in, index_in, part_in, result_in,
    e_high, e_low, h_high, h_low, part, result,
    terms, terms_in,
    local_sem, halo_send, halo_recv, terms_send, terms_recv, inv_send, inv_recv,
):
    width = loads.shape[1]
    coarse = inverse.shape[0]
    rows = inverse_parts.shape[2]
    g = lax.axis_index("grp")
    b = lax.axis_index("sub")
    grp_peers = [lax.rem(g + k, n_grp) for k in range(1, n_grp)]
    sub_peers = [lax.rem(b + k, n_sub) for k in range(1, n_sub)]
    peers = [(i, j) for i in [g] + grp_peers for j in [b] + sub_peers][1:]
    has_left = b > 0
    has_right = b < n_sub - 1
    first = pl.ds(0, RIM)
    last = pl.ds(width - RIM, RIM)

    barrier = pltpu.get_barrier_semaphore()
    for peer in peers:
        pl.semaphore_signal(barrier, inc=1, device_id=peer, device_id_type=MESH)

    def fetch(source, target, at):
        copy = pltpu.make_async_copy(source, target, local_sem.at[at])
        copy.start()
        return copy

    loads_copy = fetch(loads_hbm.at[0], loads, 0)
    basis_copy = fetch(basis_hbm.at[0], basis, 1)
    index_copy = fetch(index_hbm, index, 2)
    inverse_copy = fetch(inverse_hbm, inverse_parts.at[g, b], 3)
    neumann_copy = fetch(neumann_hbm.at[0], neumann, 4)
    schur_copy = fetch(schur_hbm.at[0], schur, 5)

    def remote(source, target, send, recv, device):
        return pltpu.make_async_remote_copy(
            src_ref=source, dst_ref=target, send_sem=send, recv_sem=recv,
            device_id=device, device_id_type=MESH,
        )

    left_id = (g, lax.max(b - 1, 0))
    right_id = (g, lax.min(b + 1, n_sub - 1))

    def halo(lower, upper, landing, at):
        to_right = remote(upper, landing.at[0], halo_send.at[at, 0], halo_recv.at[at, 0], right_id)
        to_left = remote(lower, landing.at[1], halo_send.at[at, 1], halo_recv.at[at, 1], left_id)

        def start():
            pl.when(has_right)(lambda: to_right.start())
            pl.when(has_left)(lambda: to_left.start())

        def wait_recv():
            pl.when(has_left)(lambda: to_right.wait_recv())
            pl.when(has_right)(lambda: to_left.wait_recv())

        def wait_send():
            pl.when(has_right)(lambda: to_right.wait_send())
            pl.when(has_left)(lambda: to_left.wait_send())

        return start, wait_recv, wait_send

    def clear(slot):
        loads_in[slot] = jnp.zeros(loads_in.shape[1:], F32)
        basis_in[slot] = jnp.zeros(basis_in.shape[1:], F32)
        index_in[slot] = jnp.zeros(index_in.shape[1:], jnp.int32)
        part_in[slot] = jnp.zeros(part_in.shape[1:], F32)
        result_in[slot] = jnp.zeros(result_in.shape[1:], F32)

    pl.when(jnp.logical_not(has_left))(lambda: clear(0))
    pl.when(jnp.logical_not(has_right))(lambda: clear(1))

    loads_halo = halo(loads.at[:, first], loads.at[:, last], loads_in, 0)
    basis_halo = halo(basis.at[:, first], basis.at[:, last], basis_in, 1)
    index_halo = halo(index, index, index_in, 2)
    part_halo = halo(part.at[:, first], part.at[:, last], part_in, 3)
    result_halo = halo(result.at[:, first], result.at[:, last], result_in, 4)

    loads_copy.wait()
    pl.semaphore_wait(barrier, n_grp * n_sub - 1)
    loads_halo[0]()
    index_copy.wait()
    index_halo[0]()
    basis_copy.wait()
    basis_halo[0]()
    inverse_copy.wait()
    inv_all = [
        remote(inverse_parts.at[g, b], inverse_parts.at[g, b], inv_send.at[k], inv_recv.at[k], peer)
        for k, peer in enumerate(peers)
    ]
    for copy in inv_all:
        copy.start()

    def expand(index_row, functions):
        place = lax.broadcasted_iota(jnp.int32, (coarse, index_row.shape[1]), 0)
        chosen = jnp.where(place == index_row, 1.0, 0.0).astype(BF16)
        high, low = split(functions)
        return dot(chosen, high) + dot(chosen, low)

    columns = lax.broadcasted_iota(jnp.int32, (1, width), 1)
    shared = ((columns < RIM) & has_left) | ((columns >= width - RIM) & has_right)
    weights = jnp.where(shared, 0.5, 1.0).astype(F32)

    expanded = expand(index[...], basis[...])
    high, low = split(expanded)
    e_high[...] = high
    e_low[...] = low

    loads_halo[1]()

    def assembled(field, landed):
        return jnp.concatenate(
            [field[:, :RIM] + landed[0], field[:, RIM : width - RIM], field[:, width - RIM :] + landed[1]], axis=1
        )

    force = assembled(loads[...], loads_in)
    weighted = weights * force
    terms[...] = thin_dot(weighted, e_high[...], e_low[...], NT)
    to_all = [
        remote(terms, terms_in.at[k], terms_send, terms_recv, peer) for k, peer in enumerate(peers)
    ]
    for copy in to_all:
        copy.start()

    neumann_copy.wait()
    rounded = weighted.astype(BF16)

    def neumann_columns(at, size):
        product = dot(rounded, neumann[:, at : at + size])
        here = weighted[:, at : at + size]
        part[:, at : at + size] = weights[:, at : at + size] * (0.25 * here + 0.0625 * product)

    neumann_columns(0, RIM)
    neumann_columns(width - RIM, RIM)
    part_halo[0]()

    neumann_columns(RIM, width - 2 * RIM)

    basis_halo[1]()
    index_halo[1]()
    own = weights * (e_high[...].astype(F32) + e_low[...].astype(F32))
    from_left = own[:, :RIM] + 0.5 * expand(index_in[0], basis_in[0])
    from_right = own[:, width - RIM :] + 0.5 * expand(index_in[1], basis_in[1])
    f_high, f_low = split(jnp.concatenate([from_left, own[:, RIM : width - RIM], from_right], axis=1))
    for copy in inv_all:
        copy.wait_recv()
    for i in range(n_grp):
        for j in range(n_sub):
            at = (i * n_sub + j) * rows
            inverse[at : at + rows, :] = inverse_parts[i, j]
    i_high, i_low = split(inverse[...])
    h = dot(i_high, f_high) + dot(i_high, f_low) + dot(i_low, f_high)
    high, low = split(h)
    h_high[...] = high
    h_low[...] = low

    part_halo[1]()
    base = assembled(part[...], part_in)

    pltpu.make_async_copy(terms_in, terms_in, terms_recv).wait()
    total = terms[...] + jnp.sum(terms_in[...], axis=0)
    found = base + thin_dot(total, h_high[...], h_low[...])
    solution[0] = found

    schur_copy.wait()
    rounded_solution = found.astype(BF16)

    def schur_columns(at, size):
        product = dot(rounded_solution, schur[:, at : at + size])
        return 4.0 * found[:, at : at + size] + product

    low_rim = schur_columns(0, RIM)
    high_rim = schur_columns(width - RIM, RIM)
    result[:, :RIM] = low_rim
    result[:, width - RIM :] = high_rim
    result_halo[0]()
    residual[0, :, RIM : width - RIM] = force[:, RIM : width - RIM] - schur_columns(RIM, width - 2 * RIM)
    for copy in inv_all + to_all:
        copy.wait_send()
    for each in (loads_halo, basis_halo, index_halo, part_halo):
        each[2]()
    result_halo[1]()
    residual[0, :, :RIM] = force[:, :RIM] - (low_rim + result_in[0])
    residual[0, :, width - RIM :] = force[:, width - RIM :] - (high_rim + result_in[1])
    result_halo[2]()


def store(solution, residual, solution_hbm, residual_hbm, sems):
    copies = [
        pltpu.make_async_copy(solution, solution_hbm, sems.at[0]),
        pltpu.make_async_copy(residual, residual_hbm, sems.at[1]),
    ]
    for copy in copies:
        copy.start()
    for copy in copies:
        copy.wait()


def fused(loads, schur, neumann, basis, coarse_index, coarse_inverse):
    n_grp, n_sub = lax.axis_size("grp"), lax.axis_size("sub")
    _, cases, width = loads.shape
    corners = basis.shape[1]
    rows, coarse = coarse_inverse.shape
    dma = pltpu.SemaphoreType.DMA
    field = pltpu.VMEM((cases, width), F32)
    rims = pltpu.VMEM((2, cases, RIM), F32)
    scratch = [
        field,
        pltpu.VMEM((width, width), BF16),
        pltpu.VMEM((width, width), BF16),
        pltpu.VMEM((corners, width), F32),
        pltpu.VMEM((1, corners), jnp.int32),
        pltpu.VMEM((n_grp, n_sub, rows, coarse), F32),
        pltpu.VMEM((coarse, coarse), F32),
        rims,
        pltpu.VMEM((2, corners, RIM), F32),
        pltpu.VMEM((2, 1, corners), jnp.int32),
        rims,
        rims,
        pltpu.VMEM((coarse, width), BF16),
        pltpu.VMEM((coarse, width), BF16),
        pltpu.VMEM((coarse, width), BF16),
        pltpu.VMEM((coarse, width), BF16),
        field,
        field,
        pltpu.VMEM((cases, coarse), F32),
        pltpu.VMEM((n_grp * n_sub - 1, cases, coarse), F32),
        dma((6,)),
        dma((5, 2)),
        dma((5, 2)),
        dma,
        dma,
        dma((n_grp * n_sub - 1,)),
        dma((n_grp * n_sub - 1,)),
    ]
    out = jax.ShapeDtypeStruct(loads.shape, F32)
    in_hbm = pl.BlockSpec(memory_space=pltpu.HBM)
    in_vmem = pl.BlockSpec(memory_space=pltpu.VMEM)
    found = pl.pallas_call(
        functools.partial(kernel, n_grp, n_sub),
        out_shape=(pltpu.VMEM(loads.shape, F32),) * 2,
        in_specs=[in_hbm] * 6,
        out_specs=(in_vmem, in_vmem),
        scratch_shapes=scratch,
        compiler_params=pltpu.CompilerParams(
            collective_id=0, has_side_effects=True
        ),
    )(loads, schur, neumann, basis, coarse_index, coarse_inverse)
    return pl.pallas_call(
        store,
        out_shape=(out, out),
        in_specs=[in_vmem] * 2,
        out_specs=(in_hbm, in_hbm),
        scratch_shapes=[dma((2,))],
        compiler_params=pltpu.CompilerParams(vmem_limit_bytes=1 << 20),
    )(*found)


def with_halo(x, sides, width):
    for axis, dim in sides:
        peers, length = (lax.axis_size(axis), x.shape[dim])
        up = [(i, (i + 1) % peers) for i in range(peers - 1)]
        down = [(j, i) for i, j in up]
        last = lax.slice_in_dim(x, length - width, length, axis=dim)
        first = lax.slice_in_dim(x, 0, width, axis=dim)
        before = lax.ppermute(last, axis, up)
        after = lax.ppermute(first, axis, down)
        x = jnp.concatenate([before, x, after], axis=dim)
    return x


def staged(loads, schur, neumann, basis, coarse_index, coarse_inverse):
    width = loads.shape[2]
    coarse_total = coarse_inverse.shape[1]
    high = lax.Precision.HIGHEST
    position = lax.axis_index("sub")
    final_index = lax.axis_size("sub") - 1
    columns = lax.broadcasted_iota(jnp.int32, (1, 1, width), 2)
    lower_rim = (columns < RIM) & (position > 0)
    upper_rim = (columns >= width - RIM) & (position < final_index)
    weights = jnp.where(lower_rim | upper_rim, 0.5, 1.0).astype(jnp.float32)
    selector = (
        coarse_index[0][:, None] == lax.broadcasted_iota(jnp.int32, (1, coarse_total), 1)
    ).astype(jnp.float32)

    def assemble(field):
        padded = with_halo(field, (("sub", 2),), RIM)
        from_left = padded[:, :, :RIM]
        from_right = padded[:, :, RIM + width :]
        middle = field[:, :, RIM : width - RIM]
        return jnp.concatenate(
            [field[:, :, :RIM] + from_left, middle, field[:, :, width - RIM :] + from_right], axis=2
        )

    force = assemble(loads)
    residual = force
    weighted = (weights * residual)[0]
    product = jnp.dot(weighted.astype(jnp.bfloat16), neumann[0], preferred_element_type=jnp.float32)
    neumann_part = 0.25 * weighted + 0.0625 * product
    coarse_terms = jnp.dot(weighted, basis[0].T, precision=high)
    partial_sums = jnp.dot(coarse_terms, selector, precision=high)
    owned = lax.psum_scatter(partial_sums, ("grp", "sub"), scatter_dimension=1, tiled=True)
    value_terms = jnp.dot(owned, coarse_inverse, precision=high)
    within = lax.psum(value_terms, "sub")
    coarse_value = lax.psum(within, "grp")
    picked = jnp.dot(coarse_value, selector.T, precision=high)
    combined = neumann_part + jnp.dot(picked, basis[0], precision=high)
    solution = assemble(weights * combined[None])
    product = jnp.dot(
        solution[0].astype(jnp.bfloat16), schur[0], preferred_element_type=jnp.float32
    )
    residual = force - assemble((4.0 * solution[0] + product)[None])
    return (solution, residual)


def local(loads, schur, neumann, basis, coarse_index, coarse_inverse):
    coarse_total = coarse_inverse.shape[1]
    form = fused if 4 * coarse_total * coarse_total <= GATHERED_LIMIT else staged
    return form(loads, schur, neumann, basis, coarse_index, coarse_inverse)


def solution(mesh):
    in_specs = (
        P(("grp", "sub"), None, None),
        P(("grp", "sub"), None, None),
        P(("grp", "sub"), None, None),
        P(("grp", "sub"), None, None),
        P(("grp", "sub"), None),
        P(("grp", "sub"), None),
    )
    out_specs = (P(("grp", "sub"), None, None), P(("grp", "sub"), None, None))
    return jax.shard_map(local, mesh=mesh, in_specs=in_specs, out_specs=out_specs, check_vma=False)
```

```python
import functools

import jax
import jax.numpy as jnp
from jax import lax
from jax.experimental import pallas as pl
from jax.experimental.pallas import tpu as pltpu
from jax.sharding import PartitionSpec as P

RIM = 256
MESH = pl.DeviceIdType.MESH
GATHERED_LIMIT = 1 << 20
BF16 = jnp.bfloat16
F32 = jnp.float32
NN = (((1,), (0,)), ((), ()))
NT = (((1,), (1,)), ((), ()))


def split(x):
    high = x.astype(BF16)
    return high, (x - high.astype(F32)).astype(BF16)


def dot(a, b, dims=NN):
    return lax.dot_general(a, b, dims, preferred_element_type=F32)


def thin_dot(a, b_high, b_low, dims=NN):
    rows = a.shape[0]
    high, low = split(a)
    both = dot(jnp.concatenate([high, low], axis=0), b_high, dims)
    return both[:rows] + both[rows:] + dot(high, b_low, dims)


def kernel(
    n_grp, n_sub,
    loads_hbm, schur_hbm, neumann_hbm, basis_hbm, index_hbm, inverse_hbm,
    solution, residual,
    loads, schur, neumann, basis, index, inverse_parts, inverse,
    loads_in, basis_in, index_in, part_in, result_in,
    e_high, e_low, h_high, h_low, part, result,
    terms, terms_in,
    local_sem, halo_send, halo_recv, terms_send, terms_recv, inv_send, inv_recv,
):
    width = loads.shape[1]
    coarse = inverse.shape[0]
    rows = inverse_parts.shape[2]
    g = lax.axis_index("grp")
    b = lax.axis_index("sub")
    grp_peers = [lax.rem(g + k, n_grp) for k in range(1, n_grp)]
    sub_peers = [lax.rem(b + k, n_sub) for k in range(1, n_sub)]
    peers = [(i, j) for i in [g] + grp_peers for j in [b] + sub_peers][1:]
    has_left = b > 0
    has_right = b < n_sub - 1
    first = pl.ds(0, RIM)
    last = pl.ds(width - RIM, RIM)

    barrier = pltpu.get_barrier_semaphore()
    for peer in peers:
        pl.semaphore_signal(barrier, inc=1, device_id=peer, device_id_type=MESH)

    def fetch(source, target, at):
        copy = pltpu.make_async_copy(source, target, local_sem.at[at])
        copy.start()
        return copy

    loads_copy = fetch(loads_hbm.at[0], loads, 0)
    basis_copy = fetch(basis_hbm.at[0], basis, 1)
    index_copy = fetch(index_hbm, index, 2)
    inverse_copy = fetch(inverse_hbm, inverse_parts.at[g, b], 3)
    neumann_copy = fetch(neumann_hbm.at[0], neumann, 4)
    schur_copy = fetch(schur_hbm.at[0], schur, 5)

    def remote(source, target, send, recv, device):
        return pltpu.make_async_remote_copy(
            src_ref=source, dst_ref=target, send_sem=send, recv_sem=recv,
            device_id=device, device_id_type=MESH,
        )

    left_id = (g, lax.max(b - 1, 0))
    right_id = (g, lax.min(b + 1, n_sub - 1))

    def halo(lower, upper, landing, at):
        to_right = remote(upper, landing.at[0], halo_send.at[at, 0], halo_recv.at[at, 0], right_id)
        to_left = remote(lower, landing.at[1], halo_send.at[at, 1], halo_recv.at[at, 1], left_id)

        def start():
            pl.when(has_right)(lambda: to_right.start())
            pl.when(has_left)(lambda: to_left.start())

        def wait_recv():
            pl.when(has_left)(lambda: to_right.wait_recv())
            pl.when(has_right)(lambda: to_left.wait_recv())

        def wait_send():
            pl.when(has_right)(lambda: to_right.wait_send())
            pl.when(has_left)(lambda: to_left.wait_send())

        return start, wait_recv, wait_send

    def clear(slot):
        loads_in[slot] = jnp.zeros(loads_in.shape[1:], F32)
        basis_in[slot] = jnp.zeros(basis_in.shape[1:], F32)
        index_in[slot] = jnp.zeros(index_in.shape[1:], jnp.int32)
        part_in[slot] = jnp.zeros(part_in.shape[1:], F32)
        result_in[slot] = jnp.zeros(result_in.shape[1:], F32)

    pl.when(jnp.logical_not(has_left))(lambda: clear(0))
    pl.when(jnp.logical_not(has_right))(lambda: clear(1))

    loads_halo = halo(loads.at[:, first], loads.at[:, last], loads_in, 0)
    basis_halo = halo(basis.at[:, first], basis.at[:, last], basis_in, 1)
    index_halo = halo(index, index, index_in, 2)
    part_halo = halo(part.at[:, first], part.at[:, last], part_in, 3)
    result_halo = halo(result.at[:, first], result.at[:, last], result_in, 4)

    loads_copy.wait()
    pl.semaphore_wait(barrier, n_grp * n_sub - 1)
    loads_halo[0]()
    index_copy.wait()
    index_halo[0]()
    basis_copy.wait()
    basis_halo[0]()
    inverse_copy.wait()
    inv_sub = [
        remote(inverse_parts.at[g, b], inverse_parts.at[g, b], inv_send.at[k], inv_recv.at[k], (g, peer))
        for k, peer in enumerate(sub_peers)
    ]
    for copy in inv_sub:
        copy.start()

    def expand(index_row, functions):
        place = lax.broadcasted_iota(jnp.int32, (coarse, index_row.shape[1]), 0)
        chosen = jnp.where(place == index_row, 1.0, 0.0).astype(BF16)
        high, low = split(functions)
        return dot(chosen, high) + dot(chosen, low)

    columns = lax.broadcasted_iota(jnp.int32, (1, width), 1)
    shared = ((columns < RIM) & has_left) | ((columns >= width - RIM) & has_right)
    weights = jnp.where(shared, 0.5, 1.0).astype(F32)

    expanded = expand(index[...], basis[...])
    high, low = split(expanded)
    e_high[...] = high
    e_low[...] = low

    loads_halo[1]()

    def assembled(field, landed):
        return jnp.concatenate(
            [field[:, :RIM] + landed[0], field[:, RIM : width - RIM], field[:, width - RIM :] + landed[1]], axis=1
        )

    force = assembled(loads[...], loads_in)
    weighted = weights * force
    terms[...] = thin_dot(weighted, e_high[...], e_low[...], NT)
    to_all = [
        remote(terms, terms_in.at[k], terms_send, terms_recv, peer) for k, peer in enumerate(peers)
    ]
    for copy in to_all:
        copy.start()

    for copy in inv_sub:
        copy.wait_recv()
    inv_grp = [
        remote(
            inverse_parts.at[g], inverse_parts.at[g],
            inv_send.at[n_sub - 1 + k], inv_recv.at[n_sub - 1 + k], (peer, b),
        )
        for k, peer in enumerate(grp_peers)
    ]
    for copy in inv_grp:
        copy.start()

    neumann_copy.wait()
    rounded = weighted.astype(BF16)

    def neumann_columns(at, size):
        product = dot(rounded, neumann[:, at : at + size])
        here = weighted[:, at : at + size]
        part[:, at : at + size] = weights[:, at : at + size] * (0.25 * here + 0.0625 * product)

    neumann_columns(0, RIM)
    neumann_columns(width - RIM, RIM)
    part_halo[0]()

    neumann_columns(RIM, width - 2 * RIM)

    basis_halo[1]()
    index_halo[1]()
    own = weights * (e_high[...].astype(F32) + e_low[...].astype(F32))
    from_left = own[:, :RIM] + 0.5 * expand(index_in[0], basis_in[0])
    from_right = own[:, width - RIM :] + 0.5 * expand(index_in[1], basis_in[1])
    f_high, f_low = split(jnp.concatenate([from_left, own[:, RIM : width - RIM], from_right], axis=1))
    for copy in inv_grp:
        copy.wait_recv()
    for i in range(n_grp):
        for j in range(n_sub):
            at = (i * n_sub + j) * rows
            inverse[at : at + rows, :] = inverse_parts[i, j]
    i_high, i_low = split(inverse[...])
    h = dot(i_high, f_high) + dot(i_high, f_low) + dot(i_low, f_high)
    high, low = split(h)
    h_high[...] = high
    h_low[...] = low

    part_halo[1]()
    base = assembled(part[...], part_in)

    pltpu.make_async_copy(terms_in, terms_in, terms_recv).wait()
    total = terms[...] + jnp.sum(terms_in[...], axis=0)
    found = base + thin_dot(total, h_high[...], h_low[...])
    solution[0] = found

    schur_copy.wait()
    rounded_solution = found.astype(BF16)

    def schur_columns(at, size):
        product = dot(rounded_solution, schur[:, at : at + size])
        return 4.0 * found[:, at : at + size] + product

    low_rim = schur_columns(0, RIM)
    high_rim = schur_columns(width - RIM, RIM)
    result[:, :RIM] = low_rim
    result[:, width - RIM :] = high_rim
    result_halo[0]()
    residual[0, :, RIM : width - RIM] = force[:, RIM : width - RIM] - schur_columns(RIM, width - 2 * RIM)
    for copy in inv_sub + inv_grp + to_all:
        copy.wait_send()
    for each in (loads_halo, basis_halo, index_halo, part_halo):
        each[2]()
    result_halo[1]()
    residual[0, :, :RIM] = force[:, :RIM] - (low_rim + result_in[0])
    residual[0, :, width - RIM :] = force[:, width - RIM :] - (high_rim + result_in[1])
    result_halo[2]()


def store(solution, residual, solution_hbm, residual_hbm, sems):
    copies = [
        pltpu.make_async_copy(solution, solution_hbm, sems.at[0]),
        pltpu.make_async_copy(residual, residual_hbm, sems.at[1]),
    ]
    for copy in copies:
        copy.start()
    for copy in copies:
        copy.wait()


def fused(loads, schur, neumann, basis, coarse_index, coarse_inverse):
    n_grp, n_sub = lax.axis_size("grp"), lax.axis_size("sub")
    _, cases, width = loads.shape
    corners = basis.shape[1]
    rows, coarse = coarse_inverse.shape
    dma = pltpu.SemaphoreType.DMA
    field = pltpu.VMEM((cases, width), F32)
    rims = pltpu.VMEM((2, cases, RIM), F32)
    scratch = [
        field,
        pltpu.VMEM((width, width), BF16),
        pltpu.VMEM((width, width), BF16),
        pltpu.VMEM((corners, width), F32),
        pltpu.VMEM((1, corners), jnp.int32),
        pltpu.VMEM((n_grp, n_sub, rows, coarse), F32),
        pltpu.VMEM((coarse, coarse), F32),
        rims,
        pltpu.VMEM((2, corners, RIM), F32),
        pltpu.VMEM((2, 1, corners), jnp.int32),
        rims,
        rims,
        pltpu.VMEM((coarse, width), BF16),
        pltpu.VMEM((coarse, width), BF16),
        pltpu.VMEM((coarse, width), BF16),
        pltpu.VMEM((coarse, width), BF16),
        field,
        field,
        pltpu.VMEM((cases, coarse), F32),
        pltpu.VMEM((n_grp * n_sub - 1, cases, coarse), F32),
        dma((6,)),
        dma((5, 2)),
        dma((5, 2)),
        dma,
        dma,
        dma((n_grp + n_sub - 2,)),
        dma((n_grp + n_sub - 2,)),
    ]
    out = jax.ShapeDtypeStruct(loads.shape, F32)
    in_hbm = pl.BlockSpec(memory_space=pltpu.HBM)
    in_vmem = pl.BlockSpec(memory_space=pltpu.VMEM)
    found = pl.pallas_call(
        functools.partial(kernel, n_grp, n_sub),
        out_shape=(pltpu.VMEM(loads.shape, F32),) * 2,
        in_specs=[in_hbm] * 6,
        out_specs=(in_vmem, in_vmem),
        scratch_shapes=scratch,
        compiler_params=pltpu.CompilerParams(
            collective_id=0, has_side_effects=True
        ),
    )(loads, schur, neumann, basis, coarse_index, coarse_inverse)
    return pl.pallas_call(
        store,
        out_shape=(out, out),
        in_specs=[in_vmem] * 2,
        out_specs=(in_hbm, in_hbm),
        scratch_shapes=[dma((2,))],
        compiler_params=pltpu.CompilerParams(vmem_limit_bytes=1 << 20),
    )(*found)


def with_halo(x, sides, width):
    for axis, dim in sides:
        peers, length = (lax.axis_size(axis), x.shape[dim])
        up = [(i, (i + 1) % peers) for i in range(peers - 1)]
        down = [(j, i) for i, j in up]
        last = lax.slice_in_dim(x, length - width, length, axis=dim)
        first = lax.slice_in_dim(x, 0, width, axis=dim)
        before = lax.ppermute(last, axis, up)
        after = lax.ppermute(first, axis, down)
        x = jnp.concatenate([before, x, after], axis=dim)
    return x


def staged(loads, schur, neumann, basis, coarse_index, coarse_inverse):
    width = loads.shape[2]
    coarse_total = coarse_inverse.shape[1]
    high = lax.Precision.HIGHEST
    position = lax.axis_index("sub")
    final_index = lax.axis_size("sub") - 1
    columns = lax.broadcasted_iota(jnp.int32, (1, 1, width), 2)
    lower_rim = (columns < RIM) & (position > 0)
    upper_rim = (columns >= width - RIM) & (position < final_index)
    weights = jnp.where(lower_rim | upper_rim, 0.5, 1.0).astype(jnp.float32)
    selector = (
        coarse_index[0][:, None] == lax.broadcasted_iota(jnp.int32, (1, coarse_total), 1)
    ).astype(jnp.float32)

    def assemble(field):
        padded = with_halo(field, (("sub", 2),), RIM)
        from_left = padded[:, :, :RIM]
        from_right = padded[:, :, RIM + width :]
        middle = field[:, :, RIM : width - RIM]
        return jnp.concatenate(
            [field[:, :, :RIM] + from_left, middle, field[:, :, width - RIM :] + from_right], axis=2
        )

    force = assemble(loads)
    residual = force
    weighted = (weights * residual)[0]
    product = jnp.dot(weighted.astype(jnp.bfloat16), neumann[0], preferred_element_type=jnp.float32)
    neumann_part = 0.25 * weighted + 0.0625 * product
    coarse_terms = jnp.dot(weighted, basis[0].T, precision=high)
    partial_sums = jnp.dot(coarse_terms, selector, precision=high)
    owned = lax.psum_scatter(partial_sums, ("grp", "sub"), scatter_dimension=1, tiled=True)
    value_terms = jnp.dot(owned, coarse_inverse, precision=high)
    within = lax.psum(value_terms, "sub")
    coarse_value = lax.psum(within, "grp")
    picked = jnp.dot(coarse_value, selector.T, precision=high)
    combined = neumann_part + jnp.dot(picked, basis[0], precision=high)
    solution = assemble(weights * combined[None])
    product = jnp.dot(
        solution[0].astype(jnp.bfloat16), schur[0], preferred_element_type=jnp.float32
    )
    residual = force - assemble((4.0 * solution[0] + product)[None])
    return (solution, residual)


def local(loads, schur, neumann, basis, coarse_index, coarse_inverse):
    coarse_total = coarse_inverse.shape[1]
    form = fused if 4 * coarse_total * coarse_total <= GATHERED_LIMIT else staged
    return form(loads, schur, neumann, basis, coarse_index, coarse_inverse)


def solution(mesh):
    in_specs = (
        P(("grp", "sub"), None, None),
        P(("grp", "sub"), None, None),
        P(("grp", "sub"), None, None),
        P(("grp", "sub"), None, None),
        P(("grp", "sub"), None),
        P(("grp", "sub"), None),
    )
    out_specs = (P(("grp", "sub"), None, None), P(("grp", "sub"), None, None))
    return jax.shard_map(local, mesh=mesh, in_specs=in_specs, out_specs=out_specs, check_vma=False)
```
